1024 devices in a mesh: fsdp: 128 (over z, y), tp: 8 (over x, core).
Axes of the slice: x: 4, y: 4, z: 32, core: 2. Of those that a mesh axis runs over, the one named last changes fastest.
Arguments:
- trained_units: bfloat16 [8, 128, 128, 128], P('tp', 'fsdp'), may hold values from -0.046875 to 0.046875
- unit_place: int32 [8, 128], P('tp'), may hold values from 0 to 127, each once within a row
- hidden_states: bfloat16 [4, 128, 16384], P(None, 'fsdp', 'tp'), may hold values from -6 to 6
- probes: bfloat16 [512, 16384], P(None, 'tp'), may hold values from -6 to 6
- queries: bfloat16 [4, 128, 128, 128], P(None, 'fsdp', 'tp'), may hold values from -30 to 30
- key_cache: bfloat16 [128, 8, 2048, 128], P('fsdp', 'tp'), may hold values from -6 to 6
- value_cache: bfloat16 [128, 8, 2048, 128], P('fsdp', 'tp'), may hold values from -6 to 6
- new_values: bfloat16 [4, 128, 8, 128], P(None, 'fsdp', 'tp'), may hold values from -6 to 6
- cache_lengths: int32 [128], P('fsdp'), may hold values from 2 to 2044, as said below
Outputs:
- new_keys: bfloat16 [4, 128, 8, 128], P(None, 'fsdp', 'tp')
- attended: bfloat16 [4, 128, 128, 128], P(None, 'fsdp', 'tp')
- checksum: float32 [512, 1024], P(None, 'tp')
The draws below stay inside these ranges and needn't reach their ends.
Inputs may be any that keep to these rules, and one draw needn't show every extreme that they name: Each row of unit_place names every block of its slab once. `cache_lengths`: some sequence has exactly 2044 live positions.
All inputs are finite; a program needn't handle non-finite values.
Results may differ from the reference program's by a relative error of at most 0.0051.
Values may be sent and summed in bfloat16 or wider, within the bound.
No kernel may reach another device: no remote copies, remote signals or barrier semaphores. Data moves between devices by JAX's collectives and lax.ppermute only.
A program may use at most 32 MiB of HBM per device.

```python
import jax
import jax.numpy as jnp
from jax import lax

D = 16384
QH = 128
KVH = 8
HD = 128
CHECK = 512
STEPS = 4
SEQS = 1
CACHE = 2048
UNITS = 1
ROWS = 128
N_FSDP = 128
N_TP = 8


def draw_queries(key, part):
    key = jax.random.fold_in(key, 5)
    full_shape = (STEPS, N_FSDP * SEQS, QH, HD)
    values = jnp.clip(jax.random.normal(key, full_shape, jnp.float32), -6.0, 6.0)
    return values.astype(jnp.bfloat16)


def draw_key_cache(key, part):
    key = jax.random.fold_in(key, 7)
    full_shape = (N_FSDP * SEQS, KVH, CACHE, HD)
    values = jnp.clip(jax.random.normal(key, full_shape, jnp.float32), -6.0, 6.0)
    return values.astype(jnp.bfloat16)


def draw_cache_lengths(key, part):
    key = jax.random.fold_in(key, 9)
    first_key, second_key = jax.random.split(key)
    row_total = N_FSDP * SEQS
    longest = CACHE - STEPS
    levels = jax.random.randint(first_key, (row_total,), 1, 65)
    lengths = jnp.maximum(2, longest * levels * levels // 4096)
    chosen = jax.random.randint(second_key, (), 0, row_total)
    return jnp.where(jnp.arange(row_total) == chosen, longest, lengths).astype(jnp.int32)


def level_of(rng, dims, cuts, smallest, largest):
    loudness, own = 1.0, jax.random.fold_in(rng, 6)
    for position, blocks in cuts:
        heights = jnp.exp(jax.random.uniform(jax.random.fold_in(own, position), (blocks,), jnp.float32, smallest / len(cuts), largest / len(cuts)))
        loudness = loudness * jnp.repeat(heights, dims[position] // blocks).reshape([-1 if axis == position else 1 for axis in range(len(dims))])
    return loudness


def normal_values(stream_key, extent, spread, limit, cuts=(), held_as=jnp.bfloat16):
    array = jax.random.normal(stream_key, extent, jnp.float32) * spread
    if len(cuts) > 0:
        array = level_of(stream_key, extent, cuts, -0.22, 0.18) * array
    return jnp.clip(array, min=-limit, max=limit).astype(held_as)


def setup_inputs(seed: int = 0) -> dict:
    arg_keys = jax.random.split(jax.random.key(seed), 10)
    return {
        "trained_units": normal_values(arg_keys[0], (N_TP, N_FSDP * UNITS, HD, HD), D ** -0.5, 0.046875, ((0, 8), (1, 128))),
        "unit_place": jax.vmap(lambda own: jax.random.permutation(own, N_FSDP * UNITS))(jax.random.split(arg_keys[1], N_TP)).reshape((N_TP, N_FSDP * UNITS)).astype(jnp.int32),
        "hidden_states": normal_values(arg_keys[2], (STEPS, ROWS, D), 1.0, 6.0, ((1, 128), (2, 8))),
        "probes": normal_values(arg_keys[3], (CHECK, D), 1.0, 6.0, ((1, 8),)),
        "queries": draw_queries(jax.random.fold_in(arg_keys[9], 71), 0),
        "key_cache": draw_key_cache(jax.random.fold_in(arg_keys[9], 71), 0),
        "value_cache": normal_values(arg_keys[6], (ROWS, KVH, CACHE, HD), 1.0, 6.0, ((0, 128), (1, 8))),
        "new_values": normal_values(arg_keys[7], (STEPS, ROWS, KVH, HD), 1.0, 6.0, ((1, 128), (2, 8))),
        "cache_lengths": draw_cache_lengths(jax.random.fold_in(arg_keys[9], 71), 0),
    }


ROPE_BASE = 500000.0


def rotate(vectors, positions):
    half_size = vectors.shape[-1] // 2
    frequency = ROPE_BASE ** (-jnp.arange(half_size, dtype=jnp.float32) * 2.0 / vectors.shape[-1])
    angles = positions.astype(jnp.float32)[..., None] * frequency
    cosine = jnp.cos(angles)
    sine_wave = jnp.sin(angles)
    first_half = vectors[..., :half_size]
    second_half = vectors[..., half_size:]
    return jnp.concatenate([first_half * cosine - second_half * sine_wave, second_half * cosine + first_half * sine_wave], axis=-1)


def assemble(trained_units, unit_place):
    tp_count = trained_units.shape[0]
    slab_blocks = D // (tp_count * HD)
    tp_rows = jnp.arange(tp_count, dtype=jnp.int32)[:, None]
    ordered = jnp.zeros(trained_units.shape, trained_units.dtype).at[tp_rows, unit_place].set(trained_units)
    ordered = ordered.reshape(tp_count, slab_blocks, KVH, HD, HD).transpose(0, 1, 3, 2, 4)
    return ordered.reshape(D, KVH * HD)


def attend_row(packed):
    query_row, key_rows, value_rows, fresh_keys, fresh_values, length = packed
    group_size = QH // KVH
    queried = query_row.reshape(STEPS, KVH, group_size, HD).transpose(1, 0, 2, 3).reshape(KVH, STEPS * group_size, HD).astype(jnp.float32)
    score_scale = HD ** -0.5
    cache_scores = jnp.einsum("gmd,gpd->gmp", queried, key_rows.astype(jnp.float32)) * score_scale
    fresh_scores = jnp.einsum("gmd,sgd->gms", queried, fresh_keys.astype(jnp.float32)) * score_scale
    cache_spots = jnp.arange(CACHE, dtype=jnp.int32)
    cache_scores = jnp.where(cache_spots[None, None, :] < length, cache_scores, -jnp.inf)
    step_of = jnp.arange(STEPS * group_size, dtype=jnp.int32) // group_size
    fresh_steps = jnp.arange(STEPS, dtype=jnp.int32)
    fresh_scores = jnp.where(fresh_steps[None, None, :] <= step_of[None, :, None], fresh_scores, -jnp.inf)
    all_scores = jnp.concatenate([cache_scores, fresh_scores], axis=-1)
    probabilities = jax.nn.softmax(all_scores, axis=-1).astype(jnp.bfloat16)
    cache_part = jnp.einsum("gmp,gpd->gmd", probabilities[..., :CACHE].astype(jnp.float32), value_rows.astype(jnp.float32))
    fresh_part = jnp.einsum("gms,sgd->gmd", probabilities[..., CACHE:].astype(jnp.float32), fresh_values.astype(jnp.float32))
    mixed_out = cache_part + fresh_part
    return mixed_out.reshape(KVH, STEPS, group_size, HD).transpose(1, 0, 2, 3).reshape(STEPS, QH, HD).astype(jnp.bfloat16)


def reference(trained_units, unit_place, hidden_states, probes, queries, key_cache, value_cache, new_values, cache_lengths):
    weight = assemble(trained_units, unit_place)
    row_count = hidden_states.shape[1]
    raw_keys = jnp.dot(hidden_states.reshape(STEPS * row_count, D), weight, preferred_element_type=jnp.float32)
    raw_keys = raw_keys.reshape(STEPS, row_count, KVH, HD)
    positions = cache_lengths[None, :] + jnp.arange(STEPS, dtype=jnp.int32)[:, None]
    new_keys = rotate(raw_keys, positions[:, :, None]).astype(jnp.bfloat16)
    checksum = jnp.dot(probes, weight, preferred_element_type=jnp.float32)
    attended = lax.map(attend_row, (queries.transpose(1, 0, 2, 3), key_cache, value_cache, new_keys.transpose(1, 0, 2, 3), new_values.transpose(1, 0, 2, 3), cache_lengths))
    return new_keys, attended.transpose(1, 0, 2, 3), checksum
```

```python
import jax
import jax.numpy as jnp
from jax import lax
from jax.experimental import pallas as pl
from jax.experimental.pallas import tpu as pltpu
from jax.sharding import Mesh, PartitionSpec as P

ROPE_BASE = 500000.0
BF16 = jnp.bfloat16
F32 = jnp.float32

FAR, NEAR, Y, X, CORES = 8, 4, 4, 4, 2
HEADS = X * CORES
STEPS = 4
HD = 128
CHECK = 512
SHARE = CHECK // Y
SEQ_ROWS = NEAR * STEPS
GROUP_ROWS = Y * SEQ_ROWS
PACK = SHARE + 2 * SEQ_ROWS


def split_sum(value):
    high = value.astype(BF16)
    return high, (value - high.astype(F32)).astype(BF16)


def product_kernel(block_ref, head_ref, unit_ref, hidden_ref, probe_ref, out_ref, total_ref):
    step = pl.program_id(0)

    @pl.when(step == 0)
    def _():
        total_ref[...] = jnp.zeros_like(total_ref)

    head = head_ref[step]
    unit = unit_ref[0]
    total_ref[head, :GROUP_ROWS] += jnp.dot(hidden_ref[...], unit, preferred_element_type=F32)
    total_ref[head, GROUP_ROWS:] += jnp.dot(probe_ref[...], unit, preferred_element_type=F32)

    @pl.when(step == FAR - 1)
    def _():
        for y in range(Y):
            high, low = split_sum(total_ref[:, y * SEQ_ROWS : (y + 1) * SEQ_ROWS])
            out_ref[y, :, SHARE : SHARE + SEQ_ROWS] = high
            out_ref[y, :, SHARE + SEQ_ROWS :] = low
            start = GROUP_ROWS + y * SHARE
            out_ref[y, :, :SHARE] = total_ref[:, start : start + SHARE].astype(BF16)


def products(blocks, heads, units, hidden, probes):
    return pl.pallas_call(
        product_kernel,
        grid_spec=pltpu.PrefetchScalarGridSpec(
            num_scalar_prefetch=2,
            grid=(FAR,),
            in_specs=[
                pl.BlockSpec((1, HD, HD), lambda k, b, h: (k, 0, 0)),
                pl.BlockSpec((GROUP_ROWS, HD), lambda k, b, h: (0, b[k])),
                pl.BlockSpec((CHECK, HD), lambda k, b, h: (0, b[k])),
            ],
            out_specs=pl.BlockSpec((Y, HEADS, PACK, HD), lambda k, b, h: (0, 0, 0, 0)),
            scratch_shapes=[pltpu.VMEM((HEADS, GROUP_ROWS + CHECK, HD), F32)],
        ),
        out_shape=jax.ShapeDtypeStruct((Y, HEADS, PACK, HD), BF16),
        compiler_params=pltpu.CompilerParams(vmem_limit_bytes=24 << 20),
        cost_estimate=pl.CostEstimate(flops=2 * FAR * (GROUP_ROWS + CHECK) * HD * HD, bytes_accessed=4 << 20, transcendentals=0),
        name="products",
    )(blocks, heads, units, hidden, probes)


def cached_kernel(length_ref, query_ref, key_ref, value_ref, max_ref, total_ref, mixed_ref):
    scores = lax.dot_general(query_ref[...], key_ref[...], (((1,), (1,)), ((), ())), preferred_element_type=F32)
    spots = lax.broadcasted_iota(jnp.int32, scores.shape, 1)
    scores = jnp.where(spots < length_ref[0], scores * HD**-0.5, -jnp.inf)
    largest = jnp.max(scores, axis=1, keepdims=True)
    weights = jnp.exp(scores - largest)
    high, low = split_sum(weights)
    values = value_ref[...]
    mixed_ref[...] = jnp.dot(high, values, preferred_element_type=F32) + jnp.dot(low, values, preferred_element_type=F32)
    max_ref[...] = jnp.broadcast_to(largest, max_ref.shape)
    total_ref[...] = jnp.broadcast_to(jnp.sum(weights, axis=1, keepdims=True), total_ref.shape)


def cached_attention(lengths, queries, keys, values):
    rows, spots = queries.shape[0], keys.shape[0]
    vmem = pl.BlockSpec(memory_space=pltpu.VMEM)
    shape = jax.ShapeDtypeStruct((rows, HD), F32)
    return pl.pallas_call(
        cached_kernel,
        in_specs=[pl.BlockSpec(memory_space=pltpu.SMEM), vmem, vmem, vmem],
        out_specs=[vmem] * 3,
        out_shape=[shape] * 3,
        compiler_params=pltpu.CompilerParams(vmem_limit_bytes=24 << 20),
        cost_estimate=pl.CostEstimate(flops=6 * rows * spots * HD, bytes_accessed=4 * spots * HD, transcendentals=rows * spots),
        name="cached_attention",
    )(lengths, queries, keys, values)


def fresh_kernel(raw_ref, cosine_ref, sine_ref, query_ref, value_ref, max_ref, total_ref, mixed_ref, key_ref, out_ref):
    raw = raw_ref[...]
    turned = raw * cosine_ref[...] + pltpu.roll(raw, HD // 2, 1) * sine_ref[...]
    new_keys = turned.astype(BF16)
    key_ref[...] = new_keys[:STEPS]
    scores = lax.dot_general(query_ref[...], new_keys, (((1,), (1,)), ((), ())), preferred_element_type=F32)
    rows = lax.broadcasted_iota(jnp.int32, scores.shape, 0)
    steps = lax.broadcasted_iota(jnp.int32, scores.shape, 1)
    group = query_ref.shape[0] // STEPS
    scores = jnp.where(steps * group <= rows, scores * HD**-0.5, -jnp.inf)
    cached_max = max_ref[:, :1]
    largest = jnp.maximum(cached_max, jnp.max(scores, axis=1, keepdims=True))
    keep = jnp.exp(cached_max - largest)
    weights = jnp.exp(scores - largest)
    total = total_ref[:, :1] * keep + jnp.sum(weights, axis=1, keepdims=True)
    values = value_ref[...].astype(F32)
    mixed = mixed_ref[...] * keep
    for s in range(STEPS):
        mixed += weights[:, s : s + 1] * values[s : s + 1]
    out_ref[...] = (mixed / total).astype(BF16)


def fresh_attention(raw, cosine, sine, queries, values, cached):
    vmem = pl.BlockSpec(memory_space=pltpu.VMEM)
    return pl.pallas_call(
        fresh_kernel,
        in_specs=[vmem] * 8,
        out_specs=[vmem] * 2,
        out_shape=[jax.ShapeDtypeStruct((STEPS, HD), BF16), jax.ShapeDtypeStruct(queries.shape, BF16)],
        cost_estimate=pl.CostEstimate(flops=1 << 18, bytes_accessed=1 << 17, transcendentals=1024),
        name="fresh_attention",
    )(raw, cosine, sine, queries, values, *cached)


def spread(value, axis, copies):
    return lax.all_to_all(jnp.broadcast_to(value[None], (copies, *value.shape)), axis, 0, 0, tiled=True)


def on_device(trained_units, unit_place, hidden_states, probes, queries, key_cache, value_cache, new_values, cache_lengths):
    mine = lax.axis_index("zl") * Y + lax.axis_index("y")
    places = lax.dynamic_index_in_dim(unit_place.reshape(FAR, NEAR * Y), mine, axis=1, keepdims=False)
    units = spread(trained_units[0, 0], "zh", FAR)
    hidden = lax.all_gather(hidden_states[:, 0], "zl", axis=0)
    hidden = lax.all_gather(hidden, "y", axis=0).reshape(GROUP_ROWS, -1)

    query_rows = queries.reshape(-1, HD)
    cached = cached_attention(cache_lengths, query_rows, key_cache[0, 0], value_cache[0, 0])
    frequency = ROPE_BASE ** (-jnp.arange(HD // 2, dtype=F32) * 2.0 / HD)
    positions = cache_lengths + jnp.arange(2 * STEPS, dtype=jnp.int32)
    angles = positions.astype(F32)[:, None] * frequency
    cosine, sine = jnp.cos(angles), jnp.sin(angles)
    cosine = jnp.concatenate([cosine, cosine], axis=1)
    sine = jnp.concatenate([-sine, sine], axis=1)

    packed = products(places // HEADS, places % HEADS, units, hidden, probes)
    packed = lax.all_to_all(packed.reshape(Y * HEADS, PACK, HD), ("y", "x", "c"), 0, 0, tiled=True)
    packed = jnp.sum(packed.astype(F32), axis=0)
    raw = packed[SHARE : SHARE + SEQ_ROWS] + packed[SHARE + SEQ_ROWS :]
    share = jnp.broadcast_to(packed[None, :SHARE].astype(BF16), (NEAR, SHARE, HD))
    high, low = split_sum(raw.reshape(NEAR, STEPS, HD))
    packed = jnp.concatenate([share, high, low, jnp.zeros((NEAR, 2 * STEPS, HD), BF16)], axis=1)
    packed = lax.all_to_all(packed, "zl", 0, 0, tiled=True)
    packed = jnp.sum(packed.astype(F32), axis=0)
    raw = packed[SHARE : SHARE + STEPS] + packed[SHARE + STEPS : SHARE + 2 * STEPS]
    raw = jnp.concatenate([raw, jnp.zeros_like(raw)], axis=0)
    checksum = spread(packed[:SHARE].astype(BF16), "y", Y).reshape(CHECK, HD).astype(F32)

    new_keys, attended = fresh_attention(raw, cosine, sine, query_rows, new_values.reshape(STEPS, HD), cached)
    return new_keys.reshape(STEPS, 1, 1, HD), attended.reshape(queries.shape), checksum


def solution(mesh):
    own = Mesh(mesh.devices.reshape(FAR, NEAR, Y, X, CORES), ("zh", "zl", "y", "x", "c"))
    fsdp, tp = ("zh", "zl", "y"), ("x", "c")
    return jax.shard_map(
        on_device,
        mesh=own,
        in_specs=(
            P(tp, fsdp, None, None),
            P(tp, None),
            P(None, fsdp, tp),
            P(None, tp),
            P(None, fsdp, tp, None),
            P(fsdp, tp, None, None),
            P(fsdp, tp, None, None),
            P(None, fsdp, tp, None),
            P(fsdp),
        ),
        out_specs=(P(None, fsdp, tp, None), P(None, fsdp, tp, None), P(None, tp)),
        check_vma=False,
    )
```

```python
import jax
import jax.numpy as jnp
from jax import lax
from jax.experimental import pallas as pl
from jax.experimental.pallas import tpu as pltpu
from jax.sharding import Mesh, PartitionSpec as P

ROPE_BASE = 500000.0
BF16 = jnp.bfloat16
F32 = jnp.float32

FAR, NEAR, Y, X, CORES = 8, 4, 4, 4, 2
HEADS = X * CORES
STEPS = 4
HD = 128
CHECK = 512
SHARE = CHECK // Y
SEQ_ROWS = NEAR * STEPS
GROUP_ROWS = Y * SEQ_ROWS
PACK = SHARE + 2 * SEQ_ROWS


def split_sum(value):
    high = value.astype(BF16)
    return high, (value - high.astype(F32)).astype(BF16)


def product_kernel(block_ref, head_ref, unit_ref, hidden_ref, probe_ref, out_ref, total_ref):
    step = pl.program_id(0)

    @pl.when(step == 0)
    def _():
        total_ref[...] = jnp.zeros_like(total_ref)

    head = head_ref[step]
    unit = unit_ref[0]
    total_ref[head, :GROUP_ROWS] += jnp.dot(hidden_ref[...], unit, preferred_element_type=F32)
    total_ref[head, GROUP_ROWS:] += jnp.dot(probe_ref[...], unit, preferred_element_type=F32)

    @pl.when(step == FAR - 1)
    def _():
        for y in range(Y):
            starts = [(plane * Y + y) * STEPS for plane in range(NEAR)]
            high, low = split_sum(jnp.concatenate([total_ref[:, start : start + STEPS] for start in starts], axis=1))
            out_ref[y, :, SHARE : SHARE + SEQ_ROWS] = high
            out_ref[y, :, SHARE + SEQ_ROWS :] = low
            start = GROUP_ROWS + y * SHARE
            out_ref[y, :, :SHARE] = total_ref[:, start : start + SHARE].astype(BF16)


def products(blocks, heads, units, hidden, probes):
    return pl.pallas_call(
        product_kernel,
        grid_spec=pltpu.PrefetchScalarGridSpec(
            num_scalar_prefetch=2,
            grid=(FAR,),
            in_specs=[
                pl.BlockSpec((1, HD, HD), lambda k, b, h: (k, 0, 0)),
                pl.BlockSpec((GROUP_ROWS, HD), lambda k, b, h: (0, b[k])),
                pl.BlockSpec((CHECK, HD), lambda k, b, h: (0, b[k])),
            ],
            out_specs=pl.BlockSpec((Y, HEADS, PACK, HD), lambda k, b, h: (0, 0, 0, 0)),
            scratch_shapes=[pltpu.VMEM((HEADS, GROUP_ROWS + CHECK, HD), F32)],
        ),
        out_shape=jax.ShapeDtypeStruct((Y, HEADS, PACK, HD), BF16),
        compiler_params=pltpu.CompilerParams(vmem_limit_bytes=24 << 20),
        cost_estimate=pl.CostEstimate(flops=2 * FAR * (GROUP_ROWS + CHECK) * HD * HD, bytes_accessed=4 << 20, transcendentals=0),
        name="products",
    )(blocks, heads, units, hidden, probes)


def cached_kernel(length_ref, query_ref, key_ref, value_ref, max_ref, total_ref, mixed_ref):
    scores = lax.dot_general(query_ref[...], key_ref[...], (((1,), (1,)), ((), ())), preferred_element_type=F32)
    spots = lax.broadcasted_iota(jnp.int32, scores.shape, 1)
    scores = jnp.where(spots < length_ref[0], scores * HD**-0.5, -jnp.inf)
    largest = jnp.max(scores, axis=1, keepdims=True)
    weights = jnp.exp(scores - largest)
    high, low = split_sum(weights)
    values = value_ref[...]
    mixed_ref[...] = jnp.dot(high, values, preferred_element_type=F32) + jnp.dot(low, values, preferred_element_type=F32)
    max_ref[...] = jnp.broadcast_to(largest, max_ref.shape)
    total_ref[...] = jnp.broadcast_to(jnp.sum(weights, axis=1, keepdims=True), total_ref.shape)


def cached_attention(lengths, queries, keys, values):
    rows, spots = queries.shape[0], keys.shape[0]
    vmem = pl.BlockSpec(memory_space=pltpu.VMEM)
    shape = jax.ShapeDtypeStruct((rows, HD), F32)
    return pl.pallas_call(
        cached_kernel,
        in_specs=[pl.BlockSpec(memory_space=pltpu.SMEM), vmem, vmem, vmem],
        out_specs=[vmem] * 3,
        out_shape=[shape] * 3,
        compiler_params=pltpu.CompilerParams(vmem_limit_bytes=24 << 20),
        cost_estimate=pl.CostEstimate(flops=6 * rows * spots * HD, bytes_accessed=4 * spots * HD, transcendentals=rows * spots),
        name="cached_attention",
    )(lengths, queries, keys, values)


def fresh_kernel(raw_ref, cosine_ref, sine_ref, query_ref, value_ref, max_ref, total_ref, mixed_ref, key_ref, out_ref):
    raw = raw_ref[...]
    turned = raw * cosine_ref[...] + pltpu.roll(raw, HD // 2, 1) * sine_ref[...]
    new_keys = turned.astype(BF16)
    key_ref[...] = new_keys[:STEPS]
    scores = lax.dot_general(query_ref[...], new_keys, (((1,), (1,)), ((), ())), preferred_element_type=F32)
    rows = lax.broadcasted_iota(jnp.int32, scores.shape, 0)
    steps = lax.broadcasted_iota(jnp.int32, scores.shape, 1)
    group = query_ref.shape[0] // STEPS
    scores = jnp.where(steps * group <= rows, scores * HD**-0.5, -jnp.inf)
    cached_max = max_ref[:, :1]
    largest = jnp.maximum(cached_max, jnp.max(scores, axis=1, keepdims=True))
    keep = jnp.exp(cached_max - largest)
    weights = jnp.exp(scores - largest)
    total = total_ref[:, :1] * keep + jnp.sum(weights, axis=1, keepdims=True)
    values = value_ref[...].astype(F32)
    mixed = mixed_ref[...] * keep
    for s in range(STEPS):
        mixed += weights[:, s : s + 1] * values[s : s + 1]
    out_ref[...] = (mixed / total).astype(BF16)


def fresh_attention(raw, cosine, sine, queries, values, cached):
    vmem = pl.BlockSpec(memory_space=pltpu.VMEM)
    return pl.pallas_call(
        fresh_kernel,
        in_specs=[vmem] * 8,
        out_specs=[vmem] * 2,
        out_shape=[jax.ShapeDtypeStruct((STEPS, HD), BF16), jax.ShapeDtypeStruct(queries.shape, BF16)],
        cost_estimate=pl.CostEstimate(flops=1 << 18, bytes_accessed=1 << 17, transcendentals=1024),
        name="fresh_attention",
    )(raw, cosine, sine, queries, values, *cached)


def spread(value, axis, copies):
    return lax.all_to_all(jnp.broadcast_to(value[None], (copies, *value.shape)), axis, 0, 0, tiled=True)


def on_device(trained_units, unit_place, hidden_states, probes, queries, key_cache, value_cache, new_values, cache_lengths):
    mine = lax.axis_index("zl") * Y + lax.axis_index("y")
    places = lax.dynamic_index_in_dim(unit_place.reshape(FAR, NEAR * Y), mine, axis=1, keepdims=False)
    units = spread(trained_units[0, 0], "zh", FAR)
    hidden = lax.all_gather(hidden_states[:, 0], "y", axis=0).reshape(Y * STEPS, -1)
    hidden = lax.all_gather(hidden, "zl", axis=0).reshape(GROUP_ROWS, -1)

    query_rows = queries.reshape(-1, HD)
    cached = cached_attention(cache_lengths, query_rows, key_cache[0, 0], value_cache[0, 0])
    frequency = ROPE_BASE ** (-jnp.arange(HD // 2, dtype=F32) * 2.0 / HD)
    positions = cache_lengths + jnp.arange(2 * STEPS, dtype=jnp.int32)
    angles = positions.astype(F32)[:, None] * frequency
    cosine, sine = jnp.cos(angles), jnp.sin(angles)
    cosine = jnp.concatenate([cosine, cosine], axis=1)
    sine = jnp.concatenate([-sine, sine], axis=1)

    packed = products(places // HEADS, places % HEADS, units, hidden, probes)
    packed = lax.all_to_all(packed.reshape(Y * HEADS, PACK, HD), ("y", "x", "c"), 0, 0, tiled=True)
    packed = jnp.sum(packed.astype(F32), axis=0)
    raw = packed[SHARE : SHARE + SEQ_ROWS] + packed[SHARE + SEQ_ROWS :]
    share = jnp.broadcast_to(packed[None, :SHARE].astype(BF16), (NEAR, SHARE, HD))
    high, low = split_sum(raw.reshape(NEAR, STEPS, HD))
    packed = jnp.concatenate([share, high, low, jnp.zeros((NEAR, 2 * STEPS, HD), BF16)], axis=1)
    packed = lax.all_to_all(packed, "zl", 0, 0, tiled=True)
    packed = jnp.sum(packed.astype(F32), axis=0)
    raw = packed[SHARE : SHARE + STEPS] + packed[SHARE + STEPS : SHARE + 2 * STEPS]
    raw = jnp.concatenate([raw, jnp.zeros_like(raw)], axis=0)
    checksum = spread(packed[:SHARE].astype(BF16), "y", Y).reshape(CHECK, HD).astype(F32)

    new_keys, attended = fresh_attention(raw, cosine, sine, query_rows, new_values.reshape(STEPS, HD), cached)
    return new_keys.reshape(STEPS, 1, 1, HD), attended.reshape(queries.shape), checksum


def solution(mesh):
    own = Mesh(mesh.devices.reshape(FAR, NEAR, Y, X, CORES), ("zh", "zl", "y", "x", "c"))
    fsdp, tp = ("zh", "zl", "y"), ("x", "c")
    return jax.shard_map(
        on_device,
        mesh=own,
        in_specs=(
            P(tp, fsdp, None, None),
            P(tp, None),
            P(None, fsdp, tp),
            P(None, tp),
            P(None, fsdp, tp, None),
            P(fsdp, tp, None, None),
            P(fsdp, tp, None, None),
            P(None, fsdp, tp, None),
            P(fsdp),
        ),
        out_specs=(P(None, fsdp, tp, None), P(None, fsdp, tp, None), P(None, tp)),
        check_vma=False,
    )
```

```python
import jax
import jax.numpy as jnp
from jax import lax
from jax.experimental import pallas as pl
from jax.experimental.pallas import tpu as pltpu
from jax.sharding import Mesh, PartitionSpec as P

ROPE_BASE = 500000.0
BF16 = jnp.bfloat16
F32 = jnp.float32

FAR, NEAR, Y, X, CORES = 8, 4, 4, 4, 2
PAIR = 2
HEADS = X * CORES
STEPS = 4
HD = 128
CHECK = 512
PART = CHECK // PAIR
SHARE = PART // Y
SEQ_ROWS = NEAR * STEPS
GROUP_ROWS = Y * SEQ_ROWS
PACK = SHARE + 2 * SEQ_ROWS


def split_sum(value):
    high = value.astype(BF16)
    return high, (value - high.astype(F32)).astype(BF16)


def product_kernel(block_ref, head_ref, part_ref, unit_ref, hidden_ref, probe_ref, out_ref, total_ref):
    step = pl.program_id(0)

    @pl.when(step == 0)
    def _():
        total_ref[...] = jnp.zeros_like(total_ref)

    head = head_ref[step]
    unit = unit_ref[0]
    total_ref[head, :GROUP_ROWS] += jnp.dot(hidden_ref[...], unit, preferred_element_type=F32)
    total_ref[head, GROUP_ROWS:] += jnp.dot(probe_ref[...], unit, preferred_element_type=F32)

    @pl.when(step == FAR - 1)
    def _():
        for y in range(Y):
            high, low = split_sum(total_ref[:, y * SEQ_ROWS : (y + 1) * SEQ_ROWS])
            out_ref[y, :, SHARE : SHARE + SEQ_ROWS] = high
            out_ref[y, :, SHARE + SEQ_ROWS :] = low
            start = GROUP_ROWS + y * SHARE
            out_ref[y, :, :SHARE] = total_ref[:, start : start + SHARE].astype(BF16)


def products(blocks, heads, part, units, hidden, probes):
    return pl.pallas_call(
        product_kernel,
        grid_spec=pltpu.PrefetchScalarGridSpec(
            num_scalar_prefetch=3,
            grid=(FAR,),
            in_specs=[
                pl.BlockSpec((1, HD, HD), lambda k, b, h, part: (k, 0, 0)),
                pl.BlockSpec((GROUP_ROWS, HD), lambda k, b, h, part: (0, b[k])),
                pl.BlockSpec((PART, HD), lambda k, b, h, part: (part[0], b[k])),
            ],
            out_specs=pl.BlockSpec((Y, HEADS, PACK, HD), lambda k, b, h, part: (0, 0, 0, 0)),
            scratch_shapes=[pltpu.VMEM((HEADS, GROUP_ROWS + PART, HD), F32)],
        ),
        out_shape=jax.ShapeDtypeStruct((Y, HEADS, PACK, HD), BF16),
        compiler_params=pltpu.CompilerParams(vmem_limit_bytes=24 << 20),
        cost_estimate=pl.CostEstimate(flops=2 * FAR * (GROUP_ROWS + PART) * HD * HD, bytes_accessed=2 << 20, transcendentals=0),
        name="products",
    )(blocks, heads, part, units, hidden, probes)


def cached_kernel(length_ref, query_ref, key_ref, value_ref, max_ref, total_ref, mixed_ref):
    scores = lax.dot_general(query_ref[...], key_ref[...], (((1,), (1,)), ((), ())), preferred_element_type=F32)
    spots = lax.broadcasted_iota(jnp.int32, scores.shape, 1)
    scores = jnp.where(spots < length_ref[0], scores * HD**-0.5, -jnp.inf)
    largest = jnp.max(scores, axis=1, keepdims=True)
    weights = jnp.exp(scores - largest)
    high, low = split_sum(weights)
    values = value_ref[...]
    mixed_ref[...] = jnp.dot(high, values, preferred_element_type=F32) + jnp.dot(low, values, preferred_element_type=F32)
    max_ref[...] = jnp.broadcast_to(largest, max_ref.shape)
    total_ref[...] = jnp.broadcast_to(jnp.sum(weights, axis=1, keepdims=True), total_ref.shape)


def cached_attention(lengths, queries, keys, values):
    rows, spots = queries.shape[0], keys.shape[0]
    vmem = pl.BlockSpec(memory_space=pltpu.VMEM)
    shape = jax.ShapeDtypeStruct((rows, HD), F32)
    return pl.pallas_call(
        cached_kernel,
        in_specs=[pl.BlockSpec(memory_space=pltpu.SMEM), vmem, vmem, vmem],
        out_specs=[vmem] * 3,
        out_shape=[shape] * 3,
        compiler_params=pltpu.CompilerParams(vmem_limit_bytes=24 << 20),
        cost_estimate=pl.CostEstimate(flops=6 * rows * spots * HD, bytes_accessed=4 * spots * HD, transcendentals=rows * spots),
        name="cached_attention",
    )(lengths, queries, keys, values)


def fresh_kernel(raw_ref, cosine_ref, sine_ref, query_ref, value_ref, max_ref, total_ref, mixed_ref, key_ref, out_ref):
    raw = raw_ref[...]
    turned = raw * cosine_ref[...] + pltpu.roll(raw, HD // 2, 1) * sine_ref[...]
    new_keys = turned.astype(BF16)
    key_ref[...] = new_keys[:STEPS]
    scores = lax.dot_general(query_ref[...], new_keys, (((1,), (1,)), ((), ())), preferred_element_type=F32)
    rows = lax.broadcasted_iota(jnp.int32, scores.shape, 0)
    steps = lax.broadcasted_iota(jnp.int32, scores.shape, 1)
    group = query_ref.shape[0] // STEPS
    scores = jnp.where(steps * group <= rows, scores * HD**-0.5, -jnp.inf)
    cached_max = max_ref[:, :1]
    largest = jnp.maximum(cached_max, jnp.max(scores, axis=1, keepdims=True))
    keep = jnp.exp(cached_max - largest)
    weights = jnp.exp(scores - largest)
    total = total_ref[:, :1] * keep + jnp.sum(weights, axis=1, keepdims=True)
    values = value_ref[...].astype(F32)
    mixed = mixed_ref[...] * keep
    for s in range(STEPS):
        mixed += weights[:, s : s + 1] * values[s : s + 1]
    out_ref[...] = (mixed / total).astype(BF16)


def fresh_attention(raw, cosine, sine, queries, values, cached):
    vmem = pl.BlockSpec(memory_space=pltpu.VMEM)
    return pl.pallas_call(
        fresh_kernel,
        in_specs=[vmem] * 8,
        out_specs=[vmem] * 2,
        out_shape=[jax.ShapeDtypeStruct((STEPS, HD), BF16), jax.ShapeDtypeStruct(queries.shape, BF16)],
        cost_estimate=pl.CostEstimate(flops=1 << 18, bytes_accessed=1 << 17, transcendentals=1024),
        name="fresh_attention",
    )(raw, cosine, sine, queries, values, *cached)


def spread(value, axis, copies):
    return lax.all_to_all(jnp.broadcast_to(value[None], (copies, *value.shape)), axis, 0, 0, tiled=True)


def on_device(trained_units, unit_place, hidden_states, probes, queries, key_cache, value_cache, new_values, cache_lengths):
    mine = lax.axis_index("zl") * Y + lax.axis_index("y")
    places = lax.dynamic_index_in_dim(unit_place.reshape(FAR, NEAR * Y), mine, axis=1, keepdims=False)
    hidden = spread(hidden_states[:, 0], "zl", NEAR)
    own_unit, hidden = lax.optimization_barrier((trained_units[0, 0], hidden))
    units = spread(own_unit, ("zf", "zn"), FAR)
    hidden = lax.all_gather(hidden.reshape(SEQ_ROWS, -1), "y", axis=0).reshape(GROUP_ROWS, -1)

    query_rows = queries.reshape(-1, HD)
    cached = cached_attention(cache_lengths, query_rows, key_cache[0, 0], value_cache[0, 0])
    frequency = ROPE_BASE ** (-jnp.arange(HD // 2, dtype=F32) * 2.0 / HD)
    positions = cache_lengths + jnp.arange(2 * STEPS, dtype=jnp.int32)
    angles = positions.astype(F32)[:, None] * frequency
    cosine, sine = jnp.cos(angles), jnp.sin(angles)
    cosine = jnp.concatenate([cosine, cosine], axis=1)
    sine = jnp.concatenate([-sine, sine], axis=1)

    packed = products(places // HEADS, places % HEADS, lax.axis_index("zn")[None], units, hidden, probes)
    packed = lax.all_to_all(packed.reshape(Y * HEADS, PACK, HD), ("y", "x", "c"), 0, 0, tiled=True)
    packed = jnp.sum(packed.astype(F32), axis=0)
    raw = packed[SHARE : SHARE + SEQ_ROWS] + packed[SHARE + SEQ_ROWS :]
    share = jnp.broadcast_to(packed[None, :SHARE].astype(BF16), (NEAR, SHARE, HD))
    high, low = split_sum(raw.reshape(NEAR, STEPS, HD))
    packed = jnp.concatenate([share, high, low, jnp.zeros((NEAR, 2 * STEPS, HD), BF16)], axis=1)
    packed = lax.all_to_all(packed, "zl", 0, 0, tiled=True)
    packed = jnp.sum(packed.astype(F32), axis=0)
    raw = packed[SHARE : SHARE + STEPS] + packed[SHARE + STEPS : SHARE + 2 * STEPS]
    raw = jnp.concatenate([raw, jnp.zeros_like(raw)], axis=0)
    checksum = spread(packed[:SHARE].astype(BF16), ("zn", "y"), PAIR * Y).reshape(CHECK, HD).astype(F32)

    new_keys, attended = fresh_attention(raw, cosine, sine, query_rows, new_values.reshape(STEPS, HD), cached)
    return new_keys.reshape(STEPS, 1, 1, HD), attended.reshape(queries.shape), checksum


def solution(mesh):
    own = Mesh(mesh.devices.reshape(-1, PAIR, NEAR, Y, X, CORES), ("zf", "zn", "zl", "y", "x", "c"))
    fsdp, tp = ("zf", "zn", "zl", "y"), ("x", "c")
    return jax.shard_map(
        on_device,
        mesh=own,
        in_specs=(
            P(tp, fsdp, None, None),
            P(tp, None),
            P(None, fsdp, tp),
            P(None, tp),
            P(None, fsdp, tp, None),
            P(fsdp, tp, None, None),
            P(fsdp, tp, None, None),
            P(None, fsdp, tp, None),
            P(fsdp),
        ),
        out_specs=(P(None, fsdp, tp, None), P(None, fsdp, tp, None), P(None, tp)),
        check_vma=False,
    )
```

```python
import jax
import jax.numpy as jnp
from jax import lax
from jax.experimental import pallas as pl
from jax.experimental.pallas import tpu as pltpu
from jax.sharding import Mesh, PartitionSpec as P

ROPE_BASE = 500000.0
BF16 = jnp.bfloat16
F32 = jnp.float32

FAR, NEAR, Y, X, CORES = 8, 4, 4, 4, 2
HEADS = X * CORES
STEPS = 4
HD = 128
CHECK = 512
SHARE = CHECK // Y
SEQ_ROWS = NEAR * STEPS
GROUP_ROWS = Y * SEQ_ROWS
PACK = SHARE + 2 * SEQ_ROWS


def split_sum(value):
    high = value.astype(BF16)
    return high, (value - high.astype(F32)).astype(BF16)


def product_kernel(place_ref, spot_ref, unit_ref, hidden_ref, probe_ref, kept_ref, sent_ref, total_ref):
    step = pl.program_id(0)

    @pl.when(step == 0)
    def _():
        total_ref[...] = jnp.zeros_like(total_ref)

    head = lax.rem(place_ref[step * NEAR * Y + spot_ref[0]], HEADS)
    slot = lax.rem(head + spot_ref[1], CORES) * X + lax.div(head, CORES)
    unit = unit_ref[0]
    total_ref[slot, :GROUP_ROWS] += jnp.dot(hidden_ref[...], unit, preferred_element_type=F32)
    total_ref[slot, GROUP_ROWS:] += jnp.dot(probe_ref[...], unit, preferred_element_type=F32)

    @pl.when(step == FAR - 1)
    def _():
        for y in range(Y):
            starts = [(plane * Y + y) * STEPS for plane in range(NEAR)]
            tokens = jnp.concatenate([total_ref[:, start : start + STEPS] for start in starts], axis=1)
            start = GROUP_ROWS + y * SHARE
            kept_ref[y, :, :SHARE] = total_ref[:X, start : start + SHARE]
            kept_ref[y, :, SHARE:] = tokens[:X]
            high, low = split_sum(tokens[X:])
            sent_ref[y, :, :SHARE] = total_ref[X:, start : start + SHARE].astype(BF16)
            sent_ref[y, :, SHARE : SHARE + SEQ_ROWS] = high
            sent_ref[y, :, SHARE + SEQ_ROWS :] = low


def products(places, spot, units, hidden, probes):
    def block(k, place, spot):
        return 0, lax.div(place[k * NEAR * Y + spot[0]], HEADS)

    return pl.pallas_call(
        product_kernel,
        grid_spec=pltpu.PrefetchScalarGridSpec(
            num_scalar_prefetch=2,
            grid=(FAR,),
            in_specs=[
                pl.BlockSpec((1, HD, HD), lambda k, b, h: (k, 0, 0)),
                pl.BlockSpec((GROUP_ROWS, HD), block),
                pl.BlockSpec((CHECK, HD), block),
            ],
            out_specs=[
                pl.BlockSpec((Y, X, SHARE + SEQ_ROWS, HD), lambda k, b, h: (0, 0, 0, 0)),
                pl.BlockSpec((Y, X, PACK, HD), lambda k, b, h: (0, 0, 0, 0)),
            ],
            scratch_shapes=[pltpu.VMEM((HEADS, GROUP_ROWS + CHECK, HD), F32)],
        ),
        out_shape=[
            jax.ShapeDtypeStruct((Y, X, SHARE + SEQ_ROWS, HD), F32),
            jax.ShapeDtypeStruct((Y, X, PACK, HD), BF16),
        ],
        compiler_params=pltpu.CompilerParams(vmem_limit_bytes=24 << 20),
        cost_estimate=pl.CostEstimate(flops=2 * FAR * (GROUP_ROWS + CHECK) * HD * HD, bytes_accessed=4 << 20, transcendentals=0),
        name="products",
    )(places, spot, units, hidden, probes)


def join_kernel(kept_ref, sent_ref, out_ref):
    sent = sent_ref[...].astype(F32)
    out_ref[:, :, :SHARE] = (kept_ref[:, :, :SHARE] + sent[:, :, :SHARE]).astype(BF16)
    tokens = kept_ref[:, :, SHARE:] + sent[:, :, SHARE : SHARE + SEQ_ROWS] + sent[:, :, SHARE + SEQ_ROWS :]
    high, low = split_sum(tokens)
    out_ref[:, :, SHARE : SHARE + SEQ_ROWS] = high
    out_ref[:, :, SHARE + SEQ_ROWS :] = low


def join_cores(kept, sent):
    return pl.pallas_call(
        join_kernel,
        grid=(Y,),
        in_specs=[
            pl.BlockSpec((1, X, SHARE + SEQ_ROWS, HD), lambda y: (y, 0, 0, 0)),
            pl.BlockSpec((1, X, PACK, HD), lambda y: (y, 0, 0, 0)),
        ],
        out_specs=pl.BlockSpec((1, X, PACK, HD), lambda y: (y, 0, 0, 0)),
        out_shape=jax.ShapeDtypeStruct((Y, X, PACK, HD), BF16),
        compiler_params=pltpu.CompilerParams(vmem_limit_bytes=24 << 20),
        cost_estimate=pl.CostEstimate(flops=1 << 20, bytes_accessed=3 << 20, transcendentals=0),
        name="join_cores",
    )(kept, sent)


def cached_kernel(length_ref, query_ref, key_ref, value_ref, max_ref, total_ref, mixed_ref):
    scores = lax.dot_general(query_ref[...], key_ref[...], (((1,), (1,)), ((), ())), preferred_element_type=F32)
    spots = lax.broadcasted_iota(jnp.int32, scores.shape, 1)
    scores = jnp.where(spots < length_ref[0], scores * HD**-0.5, -jnp.inf)
    largest = jnp.max(scores, axis=1, keepdims=True)
    weights = jnp.exp(scores - largest)
    high, low = split_sum(weights)
    values = value_ref[...]
    mixed_ref[...] = jnp.dot(high, values, preferred_element_type=F32) + jnp.dot(low, values, preferred_element_type=F32)
    max_ref[...] = jnp.broadcast_to(largest, max_ref.shape)
    total_ref[...] = jnp.broadcast_to(jnp.sum(weights, axis=1, keepdims=True), total_ref.shape)


def cached_attention(lengths, queries, keys, values):
    rows, spots = queries.shape[0], keys.shape[0]
    vmem = pl.BlockSpec(memory_space=pltpu.VMEM)
    shape = jax.ShapeDtypeStruct((rows, HD), F32)
    return pl.pallas_call(
        cached_kernel,
        in_specs=[pl.BlockSpec(memory_space=pltpu.SMEM), vmem, vmem, vmem],
        out_specs=[vmem] * 3,
        out_shape=[shape] * 3,
        compiler_params=pltpu.CompilerParams(vmem_limit_bytes=24 << 20),
        cost_estimate=pl.CostEstimate(flops=6 * rows * spots * HD, bytes_accessed=4 * spots * HD, transcendentals=rows * spots),
        name="cached_attention",
    )(lengths, queries, keys, values)


def fresh_kernel(raw_ref, cosine_ref, sine_ref, query_ref, value_ref, max_ref, total_ref, mixed_ref, key_ref, out_ref):
    raw = raw_ref[...]
    turned = raw * cosine_ref[...] + pltpu.roll(raw, HD // 2, 1) * sine_ref[...]
    new_keys = turned.astype(BF16)
    key_ref[...] = new_keys[:STEPS]
    scores = lax.dot_general(query_ref[...], new_keys, (((1,), (1,)), ((), ())), preferred_element_type=F32)
    rows = lax.broadcasted_iota(jnp.int32, scores.shape, 0)
    steps = lax.broadcasted_iota(jnp.int32, scores.shape, 1)
    group = query_ref.shape[0] // STEPS
    scores = jnp.where(steps * group <= rows, scores * HD**-0.5, -jnp.inf)
    cached_max = max_ref[:, :1]
    largest = jnp.maximum(cached_max, jnp.max(scores, axis=1, keepdims=True))
    keep = jnp.exp(cached_max - largest)
    weights = jnp.exp(scores - largest)
    total = total_ref[:, :1] * keep + jnp.sum(weights, axis=1, keepdims=True)
    values = value_ref[...].astype(F32)
    mixed = mixed_ref[...] * keep
    for s in range(STEPS):
        mixed += weights[:, s : s + 1] * values[s : s + 1]
    out_ref[...] = (mixed / total).astype(BF16)


def fresh_attention(raw, cosine, sine, queries, values, cached):
    vmem = pl.BlockSpec(memory_space=pltpu.VMEM)
    return pl.pallas_call(
        fresh_kernel,
        in_specs=[vmem] * 8,
        out_specs=[vmem] * 2,
        out_shape=[jax.ShapeDtypeStruct((STEPS, HD), BF16), jax.ShapeDtypeStruct(queries.shape, BF16)],
        cost_estimate=pl.CostEstimate(flops=1 << 18, bytes_accessed=1 << 17, transcendentals=1024),
        name="fresh_attention",
    )(raw, cosine, sine, queries, values, *cached)


def spread(value, axis, copies):
    return lax.all_to_all(jnp.broadcast_to(value[None], (copies, *value.shape)), axis, 0, 0, tiled=True)


def on_device(trained_units, unit_place, hidden_states, probes, queries, key_cache, value_cache, new_values, cache_lengths):
    spot = lax.axis_index("zl") * Y + lax.axis_index("y")
    hidden = spread(hidden_states[:, 0], ("zl", "y"), NEAR * Y).reshape(GROUP_ROWS, -1)
    units = lax.all_gather(trained_units[0, 0], "zh", axis=0)

    query_rows = queries.reshape(-1, HD)
    cached = cached_attention(cache_lengths, query_rows, key_cache[0, 0], value_cache[0, 0])
    frequency = ROPE_BASE ** (-jnp.arange(HD // 2, dtype=F32) * 2.0 / HD)
    positions = cache_lengths + jnp.arange(2 * STEPS, dtype=jnp.int32)
    angles = positions.astype(F32)[:, None] * frequency
    cosine, sine = jnp.cos(angles), jnp.sin(angles)
    cosine = jnp.concatenate([cosine, cosine], axis=1)
    sine = jnp.concatenate([-sine, sine], axis=1)

    spot = jnp.stack([spot, lax.axis_index("c")])
    kept, sent = products(unit_place[0], spot, units, hidden, probes)
    sent = lax.ppermute(sent, "c", [(core, CORES - 1 - core) for core in range(CORES)])
    packed = join_cores(kept, sent)
    packed = lax.all_to_all(packed.reshape(Y * X, PACK, HD), ("y", "x"), 0, 0, tiled=True)
    packed = jnp.sum(packed.astype(F32), axis=0)
    raw = packed[SHARE : SHARE + SEQ_ROWS] + packed[SHARE + SEQ_ROWS :]
    share = jnp.broadcast_to(packed[None, :SHARE].astype(BF16), (NEAR, SHARE, HD))
    high, low = split_sum(raw.reshape(NEAR, STEPS, HD))
    packed = jnp.concatenate([share, high, low, jnp.zeros((NEAR, 2 * STEPS, HD), BF16)], axis=1)
    packed = lax.all_to_all(packed, "zl", 0, 0, tiled=True)
    packed = jnp.sum(packed.astype(F32), axis=0)
    raw = packed[SHARE : SHARE + STEPS] + packed[SHARE + STEPS : SHARE + 2 * STEPS]
    raw = jnp.concatenate([raw, jnp.zeros_like(raw)], axis=0)
    checksum = spread(packed[:SHARE].astype(BF16), "y", Y).reshape(CHECK, HD).astype(F32)

    new_keys, attended = fresh_attention(raw, cosine, sine, query_rows, new_values.reshape(STEPS, HD), cached)
    return new_keys.reshape(STEPS, 1, 1, HD), attended.reshape(queries.shape), checksum


def solution(mesh):
    own = Mesh(mesh.devices.reshape(FAR, NEAR, Y, X, CORES), ("zh", "zl", "y", "x", "c"))
    fsdp, tp = ("zh", "zl", "y"), ("x", "c")
    return jax.shard_map(
        on_device,
        mesh=own,
        in_specs=(
            P(tp, fsdp, None, None),
            P(tp, None),
            P(None, fsdp, tp),
            P(None, tp),
            P(None, fsdp, tp, None),
            P(fsdp, tp, None, None),
            P(fsdp, tp, None, None),
            P(None, fsdp, tp, None),
            P(fsdp),
        ),
        out_specs=(P(None, fsdp, tp, None), P(None, fsdp, tp, None), P(None, tp)),
        check_vma=False,
    )
```
